32 devices in a mesh: dp: 4 (over y, x), expert: 4 (over z), tensor: 2 (over core).
Axes of the slice: x: 2, y: 2, z: 4, core: 2. Of those that a mesh axis runs over, the one named last changes fastest.
Arguments:
- tokens: bfloat16 [2048, 2048], P(('dp', 'expert'), 'tensor'), may hold values from -6 to 6
- expert_ids: int32 [2048, 8], P(('dp', 'expert')), may hold values from 0 to 127, as said below
- route_weight: float32 [2048, 8], P(('dp', 'expert')), may hold values from 0.2 to 1
- gate_weight: bfloat16 [4, 2048, 768], P('expert', None, 'tensor'), may hold values from -0.125 to 0.125
- up_weight: bfloat16 [4, 2048, 768], P('expert', None, 'tensor'), may hold values from -0.125 to 0.125
- down_weight: bfloat16 [4, 768, 2048], P('expert', 'tensor'), may hold values from -0.21875 to 0.21875
- cotangent: bfloat16 [2048, 2048], P(('dp', 'expert'), 'tensor'), may hold values from -6 to 6
Outputs:
- mixed: bfloat16 [2048, 2048], P(('dp', 'expert'), 'tensor')
- token_grad: bfloat16 [2048, 2048], P(('dp', 'expert'), 'tensor')
- down_grad: bfloat16 [4, 768, 2048], P('expert', 'tensor', 'dp')
The draws below stay inside these ranges and needn't reach their ends.
Inputs may be any that keep to these rules, and one draw needn't show every extreme that they name: `expert_ids`: among the rows of one device, at most 12 pairs choose the same expert; in every replica some expert below 4 is chosen by exactly 12 pairs on each of the replica's 4 devices; a token's choices are distinct.
All inputs are finite; a program needn't handle non-finite values.
Results may differ from the reference program's by a relative error of at most 0.017.
Values may be sent and summed in bfloat16 or wider, within the bound.
A program may use at most 64 MiB of HBM per device.

```python
import jax
import jax.numpy as jnp
from jax import lax

D = 2048
FF = 768
EXPERTS = 128
TOPK = 8
TOK_DEV = 128
WINDOW = 4
CAP = 12
TOKENS = 2048
N_DP = 4
N_TENSOR = 2


def draw_expert_ids(key, part):
    nblk = TOKENS // TOK_DEV
    nrep = nblk // WINDOW
    per_block = TOK_DEV * TOPK
    chosen = jax.random.randint(jax.random.fold_in(key, 11), (nrep,), 0, WINDOW, dtype=jnp.int32)
    fixed = jnp.repeat(chosen, WINDOW)
    experts_row = jnp.arange(EXPERTS, dtype=jnp.int32)[None, :]
    is_fixed = experts_row == fixed[:, None]
    levels = jax.random.randint(jax.random.fold_in(key, 12), (nblk, EXPERTS), 0, 5, dtype=jnp.int32)
    weights = jnp.where(is_fixed, 0, jnp.left_shift(jnp.ones_like(levels), levels))
    rest = per_block - CAP
    base = jnp.minimum(CAP, rest * weights // jnp.sum(weights, axis=1, keepdims=True))
    base = jnp.where(is_fixed, CAP, base)
    deficit = per_block - jnp.sum(base, axis=1, keepdims=True)
    room = CAP - base
    scores = jax.random.randint(jax.random.fold_in(key, 13), (nblk, EXPERTS), 0, 1 << 20, dtype=jnp.int32) * EXPERTS + experts_row
    order = jnp.argsort(scores, axis=1)
    room_perm = jnp.take_along_axis(room, order, axis=1)
    earlier = jnp.cumsum(room_perm, axis=1) - room_perm
    added_perm = jnp.clip(deficit - earlier, 0, room_perm)
    inverse = jnp.argsort(order, axis=1)
    counts = base + jnp.take_along_axis(added_perm, inverse, axis=1)
    ends = jnp.cumsum(counts, axis=1)
    position = jnp.arange(per_block, dtype=jnp.int32)
    sequence = jnp.sum((ends[:, None, :] <= position[None, :, None]).astype(jnp.int32), axis=2)
    grid = jnp.transpose(sequence.reshape(nblk, TOPK, TOK_DEV), (0, 2, 1))
    token_scores = jax.random.randint(jax.random.fold_in(key, 14), (nblk, TOK_DEV), 0, 1 << 20, dtype=jnp.int32) * TOK_DEV + jnp.arange(TOK_DEV, dtype=jnp.int32)[None, :]
    token_order = jnp.argsort(token_scores, axis=1)
    grid = jnp.take_along_axis(grid, token_order[:, :, None], axis=1)
    choice_scores = jax.random.randint(jax.random.fold_in(key, 15), (nblk, TOK_DEV, TOPK), 0, 1 << 20, dtype=jnp.int32) * TOPK + jnp.arange(TOPK, dtype=jnp.int32)[None, None, :]
    grid = jnp.take_along_axis(grid, jnp.argsort(choice_scores, axis=2), axis=2)
    return grid.reshape(TOKENS, TOPK).astype(jnp.int32)


def steps_of(key, dims, cuts, low, largest):
    def one(dim, shards_of):
        draws = jax.random.uniform(jax.random.fold_in(jax.random.fold_in(key, 6), dim), (shards_of,), jnp.float32, low / len(cuts), largest / len(cuts))
        return jnp.repeat(jnp.exp(draws), dims[dim] // shards_of).reshape((-1,) + (1,) * (len(dims) - dim - 1))

    loudness = one(*cuts[0])
    for cut in cuts[1:]:
        loudness = loudness * one(*cut)
    return loudness


def centred(own_key, extent, width, limit, split=(), held_as=jnp.bfloat16):
    level = steps_of(own_key, extent, split, -0.22, 0.18) if split else 1.0
    array = jax.random.normal(own_key, extent, jnp.float32) * width * level
    return jnp.minimum(jnp.maximum(array, -limit), limit).astype(held_as)


def setup_inputs(seed: int = 0) -> dict:
    keys = jax.random.split(jax.random.key(seed), 8)
    return {
        "tokens": centred(keys[0], (TOKENS, D), 1.0, 6.0, ((0, 16), (1, 2))),
        "expert_ids": draw_expert_ids(jax.random.fold_in(keys[7], 71), 0),
        "route_weight": jnp.clip(0.2 + 0.8 * jax.random.uniform(keys[2], (TOKENS, TOPK), jnp.float32) ** steps_of(keys[2], (TOKENS, TOPK), ((0, 16),), -0.2, 0.2), 0.2, 1.0),
        "gate_weight": centred(keys[3], (WINDOW, D, FF), D ** -0.5, 0.125, ((0, 4), (2, 2))),
        "up_weight": centred(keys[4], (WINDOW, D, FF), D ** -0.5, 0.125, ((0, 4), (2, 2))),
        "down_weight": centred(keys[5], (WINDOW, FF, D), FF ** -0.5, 0.21875, ((0, 4), (1, 2))),
        "cotangent": centred(keys[6], (TOKENS, D), 1.0, 6.0, ((0, 16), (1, 2))),
    }


def silu_parts(gate):
    sig = jax.nn.sigmoid(gate)
    return sig, gate * sig


def block_rounded(partials):
    return jnp.sum(partials.astype(jnp.bfloat16).astype(jnp.float32), axis=0)


def reference(tokens, expert_ids, route_weight, gate_weight, up_weight, down_weight, cotangent):
    nblk = TOKENS // TOK_DEV
    per_block = TOK_DEV * TOPK
    pairs_all = TOKENS * TOPK
    width_tp = FF // N_TENSOR
    flat_ids = expert_ids.reshape(nblk, per_block)
    onehot = (flat_ids[:, :, None] == jnp.arange(WINDOW, dtype=jnp.int32)[None, None, :]).astype(jnp.int32)
    before = jnp.cumsum(onehot, axis=1) - onehot
    rank = jnp.sum(before * onehot, axis=2).astype(jnp.int32)
    inside = flat_ids < WINDOW
    row_expert = jnp.where(inside, flat_ids, WINDOW).astype(jnp.int32)
    row_rank = jnp.where(inside, rank, 0).astype(jnp.int32)
    blocks = jnp.broadcast_to(jnp.arange(nblk, dtype=jnp.int32)[:, None], (nblk, per_block))
    pair_index = jnp.arange(pairs_all, dtype=jnp.int32).reshape(nblk, per_block)
    table = jnp.full((WINDOW + 1, nblk, CAP), pairs_all, jnp.int32).at[row_expert, blocks, row_rank].set(pair_index)[:WINDOW]
    x_pairs = jnp.concatenate([jnp.repeat(tokens, TOPK, axis=0), jnp.zeros((1, D), jnp.bfloat16)], axis=0)
    scaled = (jnp.repeat(cotangent.astype(jnp.float32), TOPK, axis=0) * route_weight.reshape(pairs_all, 1)).astype(jnp.bfloat16)
    g_pairs = jnp.concatenate([scaled, jnp.zeros((1, D), jnp.bfloat16)], axis=0)

    def one_expert(items):
        w_gate, w_up, w_down, tab = items
        idx = tab.reshape(nblk * CAP)
        x_rows = x_pairs[idx]
        grad_rows = g_pairs[idx]
        gate = jnp.dot(x_rows, w_gate, preferred_element_type=jnp.float32)
        up = jnp.dot(x_rows, w_up, preferred_element_type=jnp.float32)
        sig, act = silu_parts(gate)
        hidden = (act * up).astype(jnp.bfloat16)
        rows = nblk * CAP
        hid_blocks = hidden.astype(jnp.float32).reshape(rows, N_TENSOR, width_tp)
        down_blocks = w_down.astype(jnp.float32).reshape(N_TENSOR, width_tp, D)
        out_rows = block_rounded(jnp.einsum('rtf,tfd->trd', hid_blocks, down_blocks)).astype(jnp.bfloat16)
        hidden_grad = jnp.dot(grad_rows, w_down.T, preferred_element_type=jnp.float32)
        gate_term = (hidden_grad * up * sig * (1.0 + gate * (1.0 - sig))).astype(jnp.bfloat16)
        up_term = (hidden_grad * act).astype(jnp.bfloat16)
        gt = gate_term.astype(jnp.float32).reshape(rows, N_TENSOR, width_tp)
        ut = up_term.astype(jnp.float32).reshape(rows, N_TENSOR, width_tp)
        wg = w_gate.astype(jnp.float32).reshape(D, N_TENSOR, width_tp)
        wu = w_up.astype(jnp.float32).reshape(D, N_TENSOR, width_tp)
        parts = jnp.einsum('rtf,dtf->trd', gt, wg) + jnp.einsum('rtf,dtf->trd', ut, wu)
        row_grad = block_rounded(parts).astype(jnp.bfloat16)
        per_rep = rows // N_DP
        gr = grad_rows.astype(jnp.float32).reshape(N_DP, per_rep, D)
        hr = hidden.astype(jnp.float32).reshape(N_DP, per_rep, FF)
        g_down = block_rounded(jnp.einsum('rnf,rnd->rfd', hr, gr)).astype(jnp.bfloat16)
        return out_rows, row_grad, g_down

    out_rows, row_grad, down_grad = lax.map(one_expert, (gate_weight, up_weight, down_weight, table))
    flat_tab = table.reshape(WINDOW * nblk * CAP)
    out_pairs = jnp.zeros((pairs_all + 1, D), jnp.bfloat16).at[flat_tab].set(out_rows.reshape(-1, D))
    grad_pairs = jnp.zeros((pairs_all + 1, D), jnp.bfloat16).at[flat_tab].set(row_grad.reshape(-1, D))
    out_tok = out_pairs[:pairs_all].astype(jnp.float32).reshape(TOKENS, TOPK, D)
    mixed = jnp.sum(out_tok * route_weight[:, :, None], axis=1).astype(jnp.bfloat16)
    token_grad = jnp.sum(grad_pairs[:pairs_all].astype(jnp.float32).reshape(TOKENS, TOPK, D), axis=1).astype(jnp.bfloat16)
    return mixed, token_grad, down_grad
```

```python
import functools

import jax
import jax.numpy as jnp
from jax import lax
from jax.experimental import pallas as pl
from jax.experimental.pallas import tpu as pltpu
from jax.sharding import PartitionSpec as P

EXPERTS = 128
MESH = pl.DeviceIdType.MESH
BF = jnp.bfloat16
F32 = jnp.float32


def mm(a, b):
    return lax.dot_general(a, b, (((1,), (0,)), ((), ())), preferred_element_type=F32)


def mm_nt(a, b):
    return lax.dot_general(a, b, (((1,), (1,)), ((), ())), preferred_element_type=F32)


def mm_tn(a, b):
    return lax.dot_general(a, b, (((0,), (0,)), ((), ())), preferred_element_type=F32)


def kernel(
    dims,
    ids_ref, rw_ref, tok_hbm, cot_hbm, wg_hbm, wu_hbm, wd_hbm,
    mixed_hbm, tgrad_hbm, dgrad_hbm,
    tok, cot, wg, wu, wd, coll, comb, xs, gs, xr, gr, hd, gd,
    ps_o, ps_g, pr_o, pr_g, os, rs, ret_o, ret_g, mix, tgr, dgr,
    load_sem, out_sem,
    x_ss, x_rs, g_ss, g_rs, xf_ss, xf_rs, gf_ss, gf_rs,
    hd_ss, hd_rs, gd_ss, gd_rs, ex_ss, ex_rs, ro_ss, ro_rs, rg_ss, rg_rs,
):
    n_dp, n_ex, cap, fused = dims
    d = lax.axis_index("dp")
    s = lax.axis_index("expert")
    t = lax.axis_index("tensor")
    other = 1 - t
    n_tok, choose = ids_ref.shape
    half = tok.shape[1]
    rows = n_ex * cap
    lanes = coll.shape[1]
    blk = gd.shape[2]

    def ex_peer(k):
        return {"dp": d, "expert": lax.rem(s + k, n_ex), "tensor": t}

    def dp_peer(k):
        return {"dp": lax.rem(d + k, n_dp), "expert": s, "tensor": t}

    partner = {"dp": d, "expert": s, "tensor": other}

    def block(i):
        return pl.ds(pl.multiple_of(i * cap, cap), cap)

    def half_ds(i):
        return pl.ds(pl.multiple_of(i * half, half), half)

    def remote(src, dst, ss, rs_, dev):
        return pltpu.make_async_remote_copy(
            src_ref=src, dst_ref=dst, send_sem=ss, recv_sem=rs_, device_id=dev, device_id_type=MESH
        )

    loads = [
        pltpu.make_async_copy(a, b, load_sem.at[i])
        for i, (a, b) in enumerate(
            ((tok_hbm, tok), (cot_hbm, cot), (wg_hbm.at[0], wg), (wu_hbm.at[0], wu), (wd_hbm.at[0], wd))
        )
    ]
    for c in loads:
        c.start()

    barrier = pltpu.get_barrier_semaphore()
    peers = [ex_peer(k) for k in range(1, n_ex)] + [partner]
    if fused:
        peers += [dp_peer(k) for k in range(1, n_dp)]
    for p in peers:
        pl.semaphore_signal(barrier, inc=1, device_id=p, device_id_type=MESH)

    lane = lax.broadcasted_iota(jnp.int32, (n_tok, lanes), 1)
    e_lane = jnp.zeros((n_tok, lanes), jnp.int32)
    for n in range(1, n_ex):
        e_lane = e_lane + jnp.where(lane >= n * cap, 1, 0)
    c_lane = (lane - e_lane * cap).astype(F32)
    chosen = jnp.zeros((n_tok, lanes), F32)
    wsum = jnp.zeros((n_tok, lanes), F32)
    for k in range(choose):
        hit = ids_ref[:, k : k + 1] == e_lane
        chosen = chosen + jnp.where(hit, 1.0, 0.0)
        wsum = wsum + jnp.where(hit, rw_ref[:, k : k + 1], 0.0)
    later = lax.broadcasted_iota(jnp.int32, (n_tok, n_tok), 0) > lax.broadcasted_iota(
        jnp.int32, (n_tok, n_tok), 1
    )
    rank = mm(jnp.where(later, 1.0, 0.0).astype(BF), chosen.astype(BF))
    sel = jnp.where(rank == c_lane, chosen, 0.0)
    wsel = sel * wsum
    coll[...] = sel.astype(BF)
    w0 = wsel.astype(BF)
    r1 = wsel - w0.astype(F32)
    w1 = r1.astype(BF)
    comb[0] = w0
    comb[1] = w1
    comb[2] = (r1 - w1.astype(F32)).astype(BF)
    sel_t = sel.T[:rows].astype(BF)
    w_slot = jnp.sum(wsel.T[:rows], axis=1, keepdims=True)

    loads[0].wait()
    xs[...] = mm(sel_t, tok[...]).astype(BF)
    xr[t, block(s), :] = xs[block(s), :]

    pl.semaphore_wait(barrier, len(peers))

    def dispatch(src, dst, ss, rs_):
        out = []
        for k in range(1, n_ex):
            c = remote(
                src.at[block(lax.rem(s + k, n_ex))], dst.at[t, block(s)], ss.at[k - 1], rs_.at[k - 1], ex_peer(k)
            )
            c.start()
            out.append(c)
        return out

    def forwarder(dst, ss, rs_):
        out = []
        for k in range(n_ex):
            b = dst.at[t, block(lax.rem(s - k + n_ex, n_ex))]
            out.append(remote(b, b, ss.at[k], rs_.at[k], partner))
        return out

    x_send = dispatch(xs, xr, x_ss, x_rs)
    x_fwd = forwarder(xr, xf_ss, xf_rs)
    x_fwd[0].start()

    loads[1].wait()
    gs[...] = (mm(sel_t, cot[...]) * w_slot).astype(BF)
    gr[t, block(s), :] = gs[block(s), :]
    g_send = dispatch(gs, gr, g_ss, g_rs)
    g_fwd = forwarder(gr, gf_ss, gf_rs)
    g_fwd[0].start()

    for k in range(1, n_ex):
        x_send[k - 1].wait_recv()
        x_fwd[k].start()
    loads[2].wait()
    loads[3].wait()
    gate = mm(xr[t], wg[half_ds(t), :])
    up = mm(xr[t], wu[half_ds(t), :])
    for c in x_fwd:
        c.wait_recv()
    gate = gate + mm(xr[other], wg[half_ds(other), :])
    up = up + mm(xr[other], wu[half_ds(other), :])
    sig = jax.nn.sigmoid(gate)
    act = gate * sig
    hidden = (act * up).astype(BF)
    hd[d] = hidden
    hd_send = []
    gd_send = []
    if fused:
        for k in range(1, n_dp):
            c = remote(hd.at[d], hd.at[d], hd_ss.at[k - 1], hd_rs.at[k - 1], dp_peer(k))
            c.start()
            hd_send.append(c)

    loads[4].wait()
    ps_o[...] = mm(hidden, wd[:, half_ds(other)]).astype(BF)
    ex_o = remote(ps_o, pr_o, ex_ss.at[0], ex_rs.at[0], partner)
    ex_o.start()
    for k in range(1, n_ex):
        g_send[k - 1].wait_recv()
        g_fwd[k].start()
    own_o = mm(hidden, wd[:, half_ds(t)]).astype(BF).astype(F32)

    def give_back(src, dst, ss, rs_):
        out = []
        for k in range(1, n_ex):
            c = remote(
                src.at[block(lax.rem(s + k, n_ex))], dst.at[block(s)], ss.at[k - 1], rs_.at[k - 1], ex_peer(k)
            )
            c.start()
            out.append(c)
        dst[block(s), :] = src[block(s), :]
        return out

    ex_o.wait_recv()
    os[...] = (own_o + pr_o[...].astype(F32)).astype(BF)
    ro_send = give_back(os, ret_o, ro_ss, ro_rs)

    hgrad = mm_nt(gr[t], wd[:, half_ds(t)])
    for c in g_fwd:
        c.wait_recv()
    if fused:
        for k in range(1, n_dp):
            at = lax.rem(d + k, n_dp) * blk
            c = remote(
                gr.at[at // half, :, pl.ds(pl.multiple_of(lax.rem(at, half), blk), blk)],
                gd.at[d],
                gd_ss.at[k - 1],
                gd_rs.at[k - 1],
                dp_peer(k),
            )
            c.start()
            gd_send.append(c)
    hgrad = hgrad + mm_nt(gr[other], wd[:, half_ds(other)])
    gate_term = (hgrad * up * sig * (1.0 + gate * (1.0 - sig))).astype(BF)
    up_term = (hgrad * act).astype(BF)

    ps_g[...] = (
        mm_nt(gate_term, wg[half_ds(other), :]) + mm_nt(up_term, wu[half_ds(other), :])
    ).astype(BF)
    ex_g = remote(ps_g, pr_g, ex_ss.at[1], ex_rs.at[1], partner)
    ex_g.start()
    own_g = (
        (mm_nt(gate_term, wg[half_ds(t), :]) + mm_nt(up_term, wu[half_ds(t), :])).astype(BF).astype(F32)
    )
    ex_g.wait_recv()
    rs[...] = (own_g + pr_g[...].astype(F32)).astype(BF)
    rg_send = give_back(rs, ret_g, rg_ss, rg_rs)

    for c in ro_send:
        c.wait_recv()
    ro = ret_o[...]
    mix[...] = (
        mm(comb[0, :, :rows], ro) + mm(comb[1, :, :rows], ro) + mm(comb[2, :, :rows], ro)
    ).astype(BF)
    out_m = pltpu.make_async_copy(mix, mixed_hbm, out_sem.at[0])
    out_m.start()

    if fused:
        at = d * blk
        total = mm_tn(
            hd[d], gr[at // half, :, pl.ds(pl.multiple_of(lax.rem(at, half), blk), blk)]
        ).astype(BF).astype(F32)
        for k in range(1, n_dp):
            hd_send[k - 1].wait_recv()
            gd_send[k - 1].wait_recv()
            src = lax.rem(d - k + n_dp, n_dp)
            total = total + mm_tn(hd[src], gd[src]).astype(BF).astype(F32)
        dgr[...] = total.astype(BF)
    else:
        for i in range(2):
            dgr[:, i * half : (i + 1) * half] = mm_tn(hidden, gr[i]).astype(BF)
    out_d = pltpu.make_async_copy(dgr, dgrad_hbm, out_sem.at[1])
    out_d.start()

    for c in rg_send:
        c.wait_recv()
    tgr[...] = mm(coll[:, :rows], ret_g[...]).astype(BF)
    out_t = pltpu.make_async_copy(tgr, tgrad_hbm, out_sem.at[2])
    out_t.start()

    for c in x_send + g_send + x_fwd + g_fwd + hd_send + gd_send + [ex_o, ex_g] + ro_send + rg_send:
        c.wait_send()
    out_m.wait()
    out_d.wait()
    out_t.wait()


def per_device(n_dp, n_ex, tokens, expert_ids, route_weight, gate_weight, up_weight, down_weight, cotangent):
    n_tok, choose = expert_ids.shape
    capacity = 3 * n_tok * choose // (2 * EXPERTS)
    cap = -(-capacity // 16) * 16
    half = tokens.shape[1]
    full = gate_weight.shape[1]
    width = gate_weight.shape[2]
    rows = n_ex * cap
    lanes = -(-rows // 128) * 128
    blk = full // n_dp
    fused = blk % 128 == 0
    d_cols = blk if fused else full
    slots = n_dp if fused else n_dp
    gd_cols = blk if fused else 128
    vm = pltpu.VMEM
    dma = pltpu.SemaphoreType.DMA
    ne, nd = n_ex - 1, max(n_dp - 1, 1)
    hbm = pl.BlockSpec(memory_space=pl.ANY)
    inv = pl.BlockSpec(memory_space=pltpu.VMEM)
    mixed, token_grad, down = pl.pallas_call(
        functools.partial(kernel, (n_dp, n_ex, cap, fused)),
        out_shape=(
            jax.ShapeDtypeStruct((n_tok, half), BF),
            jax.ShapeDtypeStruct((n_tok, half), BF),
            jax.ShapeDtypeStruct((width, d_cols), BF),
        ),
        in_specs=[inv, inv, hbm, hbm, hbm, hbm, hbm],
        out_specs=(hbm, hbm, hbm),
        scratch_shapes=[
            vm((n_tok, half), BF), vm((n_tok, half), BF),
            vm((full, width), BF), vm((full, width), BF), vm((width, full), BF),
            vm((n_tok, lanes), BF), vm((3, n_tok, lanes), BF),
            vm((rows, half), BF), vm((rows, half), BF),
            vm((2, rows, half), BF), vm((2, rows, half), BF),
            vm((slots, rows, width), BF), vm((slots, rows, gd_cols), BF),
            vm((rows, half), BF), vm((rows, half), BF), vm((rows, half), BF), vm((rows, half), BF),
            vm((rows, half), BF), vm((rows, half), BF), vm((rows, half), BF), vm((rows, half), BF),
            vm((n_tok, half), BF), vm((n_tok, half), BF), vm((width, d_cols), BF),
            dma((5,)), dma((3,)),
            dma((ne,)), dma((ne,)), dma((ne,)), dma((ne,)),
            dma((n_ex,)), dma((n_ex,)), dma((n_ex,)), dma((n_ex,)),
            dma((nd,)), dma((nd,)), dma((nd,)), dma((nd,)),
            dma((2,)), dma((2,)),
            dma((ne,)), dma((ne,)), dma((ne,)), dma((ne,)),
        ],
        compiler_params=pltpu.CompilerParams(
            collective_id=0, has_side_effects=True, vmem_limit_bytes=56 * 1024 * 1024
        ),
    )(expert_ids, route_weight, tokens, cotangent, gate_weight, up_weight, down_weight)
    if not fused:
        down = lax.psum_scatter(down, "dp", scatter_dimension=1, tiled=True)
    return mixed, token_grad, down[None]


def solution(mesh):
    placed = (
        P(("dp", "expert"), "tensor"),
        P(("dp", "expert"), None),
        P(("dp", "expert"), None),
        P("expert", None, "tensor"),
        P("expert", None, "tensor"),
        P("expert", "tensor", None),
        P(("dp", "expert"), "tensor"),
    )
    return jax.shard_map(
        functools.partial(per_device, mesh.shape["dp"], mesh.shape["expert"]),
        mesh=mesh,
        in_specs=placed,
        out_specs=(
            P(("dp", "expert"), "tensor"),
            P(("dp", "expert"), "tensor"),
            P("expert", "tensor", "dp"),
        ),
        check_vma=False,
    )
```

```python
import functools

import jax
import jax.numpy as jnp
from jax import lax
from jax.experimental import pallas as pl
from jax.experimental.pallas import tpu as pltpu
from jax.sharding import PartitionSpec as P

EXPERTS = 128
MESH = pl.DeviceIdType.MESH
BF = jnp.bfloat16
F32 = jnp.float32


def mm(a, b):
    return lax.dot_general(a, b, (((1,), (0,)), ((), ())), preferred_element_type=F32)


def mm_nt(a, b):
    return lax.dot_general(a, b, (((1,), (1,)), ((), ())), preferred_element_type=F32)


def mm_tn(a, b):
    return lax.dot_general(a, b, (((0,), (0,)), ((), ())), preferred_element_type=F32)


def kernel(
    dims,
    ids_ref, rw_ref, tok_hbm, cot_hbm, wg_hbm, wu_hbm, wd_hbm,
    mix, tgr, dgr,
    tok, cot, wg, wu, wd, coll, comb, xs, gs, xr, gr, hd, gd,
    ps_o, ps_g, pr_o, pr_g, os, rs, ret_o, ret_g,
    load_sem,
    x_ss, x_rs, g_ss, g_rs, xf_ss, xf_rs, gf_ss, gf_rs,
    hd_ss, hd_rs, gd_ss, gd_rs, ex_ss, ex_rs, ro_ss, ro_rs, rg_ss, rg_rs,
):
    n_dp, n_ex, cap, fused = dims
    d = lax.axis_index("dp")
    s = lax.axis_index("expert")
    t = lax.axis_index("tensor")
    other = 1 - t
    choose, n_tok = ids_ref.shape
    half = tok.shape[1]
    rows = n_ex * cap
    blk = gd.shape[2]

    def ex_peer(k):
        return {"dp": d, "expert": lax.rem(s + k, n_ex), "tensor": t}

    def dp_peer(k):
        return {"dp": lax.rem(d + k, n_dp), "expert": s, "tensor": t}

    partner = {"dp": d, "expert": s, "tensor": other}

    def block(i):
        return pl.ds(pl.multiple_of(i * cap, cap), cap)

    def half_ds(i):
        return pl.ds(pl.multiple_of(i * half, half), half)

    def remote(src, dst, ss, rs_, dev):
        return pltpu.make_async_remote_copy(
            src_ref=src, dst_ref=dst, send_sem=ss, recv_sem=rs_, device_id=dev, device_id_type=MESH
        )

    loads = [
        pltpu.make_async_copy(a, b, load_sem.at[i])
        for i, (a, b) in enumerate(
            ((tok_hbm, tok), (cot_hbm, cot), (wg_hbm.at[0], wg), (wu_hbm.at[0], wu), (wd_hbm.at[0], wd))
        )
    ]
    for c in loads:
        c.start()

    barrier = pltpu.get_barrier_semaphore()
    peers = [ex_peer(k) for k in range(1, n_ex)] + [partner]
    if fused:
        peers += [dp_peer(k) for k in range(1, n_dp)]
    for p in peers:
        pl.semaphore_signal(barrier, inc=1, device_id=p, device_id_type=MESH)

    row = lax.broadcasted_iota(jnp.int32, (rows, n_tok), 0)
    e_row = jnp.zeros((rows, n_tok), jnp.int32)
    for n in range(1, n_ex):
        e_row = e_row + jnp.where(row >= n * cap, 1, 0)
    c_row = (row - e_row * cap).astype(F32)
    chosen = jnp.zeros((rows, n_tok), F32)
    wsum = jnp.zeros((rows, n_tok), F32)
    for k in range(choose):
        hit = ids_ref[k : k + 1, :] == e_row
        chosen = chosen + jnp.where(hit, 1.0, 0.0)
        wsum = wsum + jnp.where(hit, rw_ref[k : k + 1, :], 0.0)
    earlier = lax.broadcasted_iota(jnp.int32, (n_tok, n_tok), 0) < lax.broadcasted_iota(
        jnp.int32, (n_tok, n_tok), 1
    )
    rank = mm(chosen.astype(BF), jnp.where(earlier, 1.0, 0.0).astype(BF))
    sel = jnp.where(rank == c_row, chosen, 0.0)
    wsel = sel * wsum
    sel_t = sel.astype(BF)
    w_slot = jnp.sum(wsel, axis=1, keepdims=True)

    loads[0].wait()
    xs[...] = mm(sel_t, tok[...]).astype(BF)
    xr[t, block(s), :] = xs[block(s), :]

    pl.semaphore_wait(barrier, len(peers))

    def dispatch(src, dst, ss, rs_):
        out = []
        for k in range(1, n_ex):
            c = remote(
                src.at[block(lax.rem(s + k, n_ex))], dst.at[t, block(s)], ss.at[k - 1], rs_.at[k - 1], ex_peer(k)
            )
            c.start()
            out.append(c)
        return out

    def forwarder(dst, ss, rs_):
        out = []
        for k in range(n_ex):
            b = dst.at[t, block(lax.rem(s - k + n_ex, n_ex))]
            out.append(remote(b, b, ss.at[k], rs_.at[k], partner))
        return out

    x_send = dispatch(xs, xr, x_ss, x_rs)
    x_fwd = forwarder(xr, xf_ss, xf_rs)
    x_fwd[0].start()

    loads[1].wait()
    gs[...] = (mm(sel_t, cot[...]) * w_slot).astype(BF)
    gr[t, block(s), :] = gs[block(s), :]
    g_send = dispatch(gs, gr, g_ss, g_rs)
    g_fwd = forwarder(gr, gf_ss, gf_rs)
    g_fwd[0].start()

    coll[...] = sel.T.astype(BF)
    wcol = wsel.T
    w0 = wcol.astype(BF)
    r1 = wcol - w0.astype(F32)
    w1 = r1.astype(BF)
    comb[0] = w0
    comb[1] = w1
    comb[2] = (r1 - w1.astype(F32)).astype(BF)

    for k in range(1, n_ex):
        x_send[k - 1].wait_recv()
        x_fwd[k].start()
    loads[2].wait()
    loads[3].wait()
    gate = mm(xr[t], wg[half_ds(t), :])
    up = mm(xr[t], wu[half_ds(t), :])
    for c in x_fwd:
        c.wait_recv()
    gate = gate + mm(xr[other], wg[half_ds(other), :])
    up = up + mm(xr[other], wu[half_ds(other), :])
    sig = jax.nn.sigmoid(gate)
    act = gate * sig
    hidden = (act * up).astype(BF)
    hd[d] = hidden
    hd_send = []
    gd_send = []
    if fused:
        for k in range(1, n_dp):
            c = remote(hd.at[d], hd.at[d], hd_ss.at[k - 1], hd_rs.at[k - 1], dp_peer(k))
            c.start()
            hd_send.append(c)

    loads[4].wait()
    ps_o[...] = mm(hidden, wd[:, half_ds(other)]).astype(BF)
    ex_o = remote(ps_o, pr_o, ex_ss.at[0], ex_rs.at[0], partner)
    ex_o.start()
    for k in range(1, n_ex):
        g_send[k - 1].wait_recv()
        g_fwd[k].start()
    own_o = mm(hidden, wd[:, half_ds(t)]).astype(BF).astype(F32)

    def give_back(src, dst, ss, rs_):
        out = []
        for k in range(1, n_ex):
            c = remote(
                src.at[block(lax.rem(s + k, n_ex))], dst.at[block(s)], ss.at[k - 1], rs_.at[k - 1], ex_peer(k)
            )
            c.start()
            out.append(c)
        dst[block(s), :] = src[block(s), :]
        return out

    ex_o.wait_recv()
    os[...] = (own_o + pr_o[...].astype(F32)).astype(BF)
    ro_send = give_back(os, ret_o, ro_ss, ro_rs)

    hgrad = mm_nt(gr[t], wd[:, half_ds(t)])
    for c in g_fwd:
        c.wait_recv()
    if fused:
        for k in range(1, n_dp):
            at = lax.rem(d + k, n_dp) * blk
            c = remote(
                gr.at[at // half, :, pl.ds(pl.multiple_of(lax.rem(at, half), blk), blk)],
                gd.at[d],
                gd_ss.at[k - 1],
                gd_rs.at[k - 1],
                dp_peer(k),
            )
            c.start()
            gd_send.append(c)
    hgrad = hgrad + mm_nt(gr[other], wd[:, half_ds(other)])
    gate_term = (hgrad * up * sig * (1.0 + gate * (1.0 - sig))).astype(BF)
    up_term = (hgrad * act).astype(BF)

    ps_g[...] = (
        mm_nt(gate_term, wg[half_ds(other), :]) + mm_nt(up_term, wu[half_ds(other), :])
    ).astype(BF)
    ex_g = remote(ps_g, pr_g, ex_ss.at[1], ex_rs.at[1], partner)
    ex_g.start()
    own_g = (
        (mm_nt(gate_term, wg[half_ds(t), :]) + mm_nt(up_term, wu[half_ds(t), :])).astype(BF).astype(F32)
    )
    ex_g.wait_recv()
    rs[...] = (own_g + pr_g[...].astype(F32)).astype(BF)
    rg_send = give_back(rs, ret_g, rg_ss, rg_rs)

    for c in ro_send:
        c.wait_recv()
    ro = ret_o[...]
    mix[...] = (
        mm(comb[0], ro) + mm(comb[1], ro) + mm(comb[2], ro)
    ).astype(BF)

    if fused:
        at = d * blk
        total = mm_tn(
            hd[d], gr[at // half, :, pl.ds(pl.multiple_of(lax.rem(at, half), blk), blk)]
        ).astype(BF).astype(F32)
        for k in range(1, n_dp):
            hd_send[k - 1].wait_recv()
            gd_send[k - 1].wait_recv()
            src = lax.rem(d - k + n_dp, n_dp)
            total = total + mm_tn(hd[src], gd[src]).astype(BF).astype(F32)
        dgr[...] = total.astype(BF)
    else:
        for i in range(2):
            dgr[:, i * half : (i + 1) * half] = mm_tn(hidden, gr[i]).astype(BF)

    for c in rg_send:
        c.wait_recv()
    tgr[...] = mm(coll[...], ret_g[...]).astype(BF)

    for c in x_send + g_send + x_fwd + g_fwd + hd_send + gd_send + [ex_o, ex_g] + ro_send + rg_send:
        c.wait_send()


def write_kernel(a, b, c, a_out, b_out, c_out, sem):
    copies = [
        pltpu.make_async_copy(i, o, sem.at[k])
        for k, (i, o) in enumerate(((a, a_out), (b, b_out), (c, c_out)))
    ]
    for cp in copies:
        cp.start()
    for cp in copies:
        cp.wait()


def per_device(n_dp, n_ex, tokens, expert_ids, route_weight, gate_weight, up_weight, down_weight, cotangent):
    n_tok, choose = expert_ids.shape
    capacity = 3 * n_tok * choose // (2 * EXPERTS)
    cap = -(-capacity // 16) * 16
    half = tokens.shape[1]
    full = gate_weight.shape[1]
    width = gate_weight.shape[2]
    rows = n_ex * cap
    blk = full // n_dp
    fused = blk % 128 == 0
    d_cols = blk if fused else full
    slots = n_dp if fused else n_dp
    gd_cols = blk if fused else 128
    vm = pltpu.VMEM
    dma = pltpu.SemaphoreType.DMA
    ne, nd = n_ex - 1, max(n_dp - 1, 1)
    hbm = pl.BlockSpec(memory_space=pl.ANY)
    inv = pl.BlockSpec(memory_space=pltpu.VMEM)
    mixed, token_grad, down = pl.pallas_call(
        functools.partial(kernel, (n_dp, n_ex, cap, fused)),
        out_shape=(vm((n_tok, half), BF), vm((n_tok, half), BF), vm((width, d_cols), BF)),
        in_specs=[inv, inv, hbm, hbm, hbm, hbm, hbm],
        out_specs=(inv, inv, inv),
        scratch_shapes=[
            vm((n_tok, half), BF), vm((n_tok, half), BF),
            vm((full, width), BF), vm((full, width), BF), vm((width, full), BF),
            vm((n_tok, rows), BF), vm((3, n_tok, rows), BF),
            vm((rows, half), BF), vm((rows, half), BF),
            vm((2, rows, half), BF), vm((2, rows, half), BF),
            vm((slots, rows, width), BF), vm((slots, rows, gd_cols), BF),
            vm((rows, half), BF), vm((rows, half), BF), vm((rows, half), BF), vm((rows, half), BF),
            vm((rows, half), BF), vm((rows, half), BF), vm((rows, half), BF), vm((rows, half), BF),
            dma((5,)),
            dma((ne,)), dma((ne,)), dma((ne,)), dma((ne,)),
            dma((n_ex,)), dma((n_ex,)), dma((n_ex,)), dma((n_ex,)),
            dma((nd,)), dma((nd,)), dma((nd,)), dma((nd,)),
            dma((2,)), dma((2,)),
            dma((ne,)), dma((ne,)), dma((ne,)), dma((ne,)),
        ],
        compiler_params=pltpu.CompilerParams(
            collective_id=0, has_side_effects=True, vmem_limit_bytes=56 * 1024 * 1024
        ),
    )(expert_ids.T, route_weight.T, tokens, cotangent, gate_weight, up_weight, down_weight)
    mixed, token_grad, down = pl.pallas_call(
        write_kernel,
        out_shape=tuple(jax.ShapeDtypeStruct(a.shape, BF) for a in (mixed, token_grad, down)),
        in_specs=[inv, inv, inv],
        out_specs=(hbm, hbm, hbm),
        scratch_shapes=[dma((3,))],
    )(*(pltpu.with_memory_space_constraint(a, pltpu.VMEM) for a in (mixed, token_grad, down)))
    if not fused:
        down = lax.psum_scatter(down, "dp", scatter_dimension=1, tiled=True)
    return mixed, token_grad, down[None]


def solution(mesh):
    placed = (
        P(("dp", "expert"), "tensor"),
        P(("dp", "expert"), None),
        P(("dp", "expert"), None),
        P("expert", None, "tensor"),
        P("expert", None, "tensor"),
        P("expert", "tensor", None),
        P(("dp", "expert"), "tensor"),
    )
    return jax.shard_map(
        functools.partial(per_device, mesh.shape["dp"], mesh.shape["expert"]),
        mesh=mesh,
        in_specs=placed,
        out_specs=(
            P(("dp", "expert"), "tensor"),
            P(("dp", "expert"), "tensor"),
            P("expert", "tensor", "dp"),
        ),
        check_vma=False,
    )
```

```python
import functools

import jax
import jax.numpy as jnp
from jax import lax
from jax.experimental import pallas as pl
from jax.experimental.pallas import tpu as pltpu
from jax.sharding import PartitionSpec as P

EXPERTS = 128
MESH = pl.DeviceIdType.MESH
BF = jnp.bfloat16
F32 = jnp.float32


def mm(a, b):
    return lax.dot_general(a, b, (((1,), (0,)), ((), ())), preferred_element_type=F32)


def mm_nt(a, b):
    return lax.dot_general(a, b, (((1,), (1,)), ((), ())), preferred_element_type=F32)


def mm_tn(a, b):
    return lax.dot_general(a, b, (((0,), (0,)), ((), ())), preferred_element_type=F32)


def kernel(
    dims,
    ids_ref, rw_ref, tok_hbm, cot_hbm, wg_hbm, wu_hbm, wd_hbm,
    mix, tgr, dgr,
    tok, cot, wg, wu, wd, coll, comb, xs, gs, xp, gp, xr, gr, hd, gd,
    ps_o, ps_g, pr_o, pr_g, os, rs, ret_o, ret_g,
    load_sem,
    x_ss, x_rs, g_ss, g_rs, xf_ss, xf_rs, gf_ss, gf_rs,
    hd_ss, hd_rs, gd_ss, gd_rs, ex_ss, ex_rs, ro_ss, ro_rs, rg_ss, rg_rs,
):
    n_dp, n_ex, cap, capacity, parts, piece, fused = dims
    d = lax.axis_index("dp")
    s = lax.axis_index("expert")
    t = lax.axis_index("tensor")
    other = 1 - t
    choose, n_tok = ids_ref.shape
    half = tok.shape[1]
    rows = n_ex * cap
    blk = gd.shape[2]

    def ex_peer(k):
        return {"dp": d, "expert": lax.rem(s + k, n_ex), "tensor": t}

    def dp_peer(k):
        return {"dp": lax.rem(d + k, n_dp), "expert": s, "tensor": t}

    partner = {"dp": d, "expert": s, "tensor": other}

    def block(i):
        return pl.ds(pl.multiple_of(i * cap, cap), cap)

    def half_ds(i):
        return pl.ds(pl.multiple_of(i * half, half), half)

    def remote(src, dst, ss, rs_, dev):
        return pltpu.make_async_remote_copy(
            src_ref=src, dst_ref=dst, send_sem=ss, recv_sem=rs_, device_id=dev, device_id_type=MESH
        )

    loads = [
        pltpu.make_async_copy(a, b, load_sem.at[i])
        for i, (a, b) in enumerate(
            ((tok_hbm, tok), (cot_hbm, cot), (wg_hbm.at[0], wg), (wu_hbm.at[0], wu), (wd_hbm.at[0], wd))
        )
    ]
    for c in loads:
        c.start()

    barrier = pltpu.get_barrier_semaphore()
    peers = [ex_peer(k) for k in range(1, n_ex)] + [partner]
    if fused:
        peers += [dp_peer(k) for k in range(1, n_dp)]
    for p in peers:
        pl.semaphore_signal(barrier, inc=1, device_id=p, device_id_type=MESH)

    row = lax.broadcasted_iota(jnp.int32, (rows, n_tok), 0)
    e_row = jnp.zeros((rows, n_tok), jnp.int32)
    for n in range(1, n_ex):
        e_row = e_row + jnp.where(row >= n * cap, 1, 0)
    c_row = (row - e_row * cap).astype(F32)
    chosen = jnp.zeros((rows, n_tok), F32)
    wsum = jnp.zeros((rows, n_tok), F32)
    for k in range(choose):
        hit = ids_ref[k : k + 1, :] == e_row
        chosen = chosen + jnp.where(hit, 1.0, 0.0)
        wsum = wsum + jnp.where(hit, rw_ref[k : k + 1, :], 0.0)
    earlier = lax.broadcasted_iota(jnp.int32, (n_tok, n_tok), 0) < lax.broadcasted_iota(
        jnp.int32, (n_tok, n_tok), 1
    )
    rank = mm(chosen.astype(BF), jnp.where(earlier, 1.0, 0.0).astype(BF))
    sel = jnp.where(rank == c_row, chosen, 0.0)
    wsel = sel * wsum
    sel_t = sel.astype(BF)
    w_slot = jnp.sum(wsel, axis=1, keepdims=True)

    sel_x, w_x, back = [], [], []
    if parts:
        r_sq = lax.broadcasted_iota(jnp.int32, (rows, rows), 0)
        m_sq = lax.broadcasted_iota(jnp.int32, (rows, rows), 1)
        base = jnp.zeros((rows, rows), jnp.int32)
        for n in range(1, n_ex):
            base = base + jnp.where(m_sq >= n * cap, cap, 0)
        m_c = m_sq - base
        back.append(jnp.where((r_sq == m_sq) & (m_c < capacity), 1.0, 0.0).astype(BF))
        c_int = row - e_row * cap
        for i in range(parts):
            c_i = jnp.where(c_int >= capacity, (c_int - capacity) * parts + i, -1).astype(F32)
            s_i = jnp.where(rank == c_i, chosen, 0.0)
            sel_x.append(s_i.astype(BF))
            w_x.append(jnp.sum(s_i * wsum, axis=1, keepdims=True))
            place = base + (m_c - capacity) * parts + i
            back.append(jnp.where((m_c >= capacity) & (r_sq == place), 1.0, 0.0).astype(BF))

    def pack(src, dst, weighted):
        if not parts:
            v = mm(sel_t, src[...])
            dst[...] = (v * w_slot if weighted else v).astype(BF)
        for i in range(parts):
            here = slice(i * piece, (i + 1) * piece)
            a = mm(sel_t, src[:, here])
            b = mm(sel_x[i], src[:, parts * piece :])
            dst[:, here] = (a * w_slot + b * w_x[i] if weighted else a + b).astype(BF)

    def unpack(src, dst, h):
        v = src[h]
        if not parts:
            dst[h] = v
        else:
            dst[h, :, : parts * piece] = mm(back[0], v).astype(BF)
            tail = mm(back[1], v[:, :piece])
            for i in range(1, parts):
                tail = tail + mm(back[i + 1], v[:, i * piece : (i + 1) * piece])
            dst[h, :, parts * piece :] = tail.astype(BF)

    loads[0].wait()
    pack(tok, xs, False)
    xp[t, block(s), :] = xs[block(s), :]

    pl.semaphore_wait(barrier, len(peers))

    def dispatch(src, dst, ss, rs_):
        out = []
        for k in range(1, n_ex):
            c = remote(
                src.at[block(lax.rem(s + k, n_ex))], dst.at[t, block(s)], ss.at[k - 1], rs_.at[k - 1], ex_peer(k)
            )
            c.start()
            out.append(c)
        return out

    def forwarder(dst, ss, rs_):
        out = []
        for k in range(n_ex):
            b = dst.at[t, block(lax.rem(s - k + n_ex, n_ex))]
            out.append(remote(b, b, ss.at[k], rs_.at[k], partner))
        return out

    x_send = dispatch(xs, xp, x_ss, x_rs)
    x_fwd = forwarder(xp, xf_ss, xf_rs)
    x_fwd[0].start()

    loads[1].wait()
    pack(cot, gs, True)
    gp[t, block(s), :] = gs[block(s), :]
    g_send = dispatch(gs, gp, g_ss, g_rs)
    g_fwd = forwarder(gp, gf_ss, gf_rs)
    g_fwd[0].start()

    coll[...] = sel.T.astype(BF)
    wcol = wsel.T
    w0 = wcol.astype(BF)
    r1 = wcol - w0.astype(F32)
    w1 = r1.astype(BF)
    comb[0] = w0
    comb[1] = w1
    comb[2] = (r1 - w1.astype(F32)).astype(BF)

    for k in range(1, n_ex):
        x_send[k - 1].wait_recv()
        x_fwd[k].start()
    unpack(xp, xr, t)
    loads[2].wait()
    loads[3].wait()
    gate = mm(xr[t], wg[half_ds(t), :])
    up = mm(xr[t], wu[half_ds(t), :])
    for c in x_fwd:
        c.wait_recv()
    unpack(xp, xr, other)
    gate = gate + mm(xr[other], wg[half_ds(other), :])
    up = up + mm(xr[other], wu[half_ds(other), :])
    sig = jax.nn.sigmoid(gate)
    act = gate * sig
    hidden = (act * up).astype(BF)
    hd[d] = hidden
    hd_send = []
    gd_send = []
    if fused:
        for k in range(1, n_dp):
            c = remote(hd.at[d], hd.at[d], hd_ss.at[k - 1], hd_rs.at[k - 1], dp_peer(k))
            c.start()
            hd_send.append(c)

    loads[4].wait()
    ps_o[...] = mm(hidden, wd[:, half_ds(other)]).astype(BF)
    ex_o = remote(ps_o, pr_o, ex_ss.at[0], ex_rs.at[0], partner)
    ex_o.start()
    for k in range(1, n_ex):
        g_send[k - 1].wait_recv()
        g_fwd[k].start()
    own_o = mm(hidden, wd[:, half_ds(t)]).astype(BF).astype(F32)

    def give_back(src, dst, ss, rs_):
        out = []
        for k in range(1, n_ex):
            c = remote(
                src.at[block(lax.rem(s + k, n_ex))], dst.at[block(s)], ss.at[k - 1], rs_.at[k - 1], ex_peer(k)
            )
            c.start()
            out.append(c)
        dst[block(s), :] = src[block(s), :]
        return out

    unpack(gp, gr, t)
    ex_o.wait_recv()
    os[...] = (own_o + pr_o[...].astype(F32)).astype(BF)
    ro_send = give_back(os, ret_o, ro_ss, ro_rs)

    hgrad = mm_nt(gr[t], wd[:, half_ds(t)])
    for c in g_fwd:
        c.wait_recv()
    unpack(gp, gr, other)
    if fused:
        for k in range(1, n_dp):
            at = lax.rem(d + k, n_dp) * blk
            c = remote(
                gr.at[at // half, :, pl.ds(pl.multiple_of(lax.rem(at, half), blk), blk)],
                gd.at[d],
                gd_ss.at[k - 1],
                gd_rs.at[k - 1],
                dp_peer(k),
            )
            c.start()
            gd_send.append(c)
    hgrad = hgrad + mm_nt(gr[other], wd[:, half_ds(other)])
    gate_term = (hgrad * up * sig * (1.0 + gate * (1.0 - sig))).astype(BF)
    up_term = (hgrad * act).astype(BF)

    ps_g[...] = (
        mm_nt(gate_term, wg[half_ds(other), :]) + mm_nt(up_term, wu[half_ds(other), :])
    ).astype(BF)
    ex_g = remote(ps_g, pr_g, ex_ss.at[1], ex_rs.at[1], partner)
    ex_g.start()
    own_g = (
        (mm_nt(gate_term, wg[half_ds(t), :]) + mm_nt(up_term, wu[half_ds(t), :])).astype(BF).astype(F32)
    )
    ex_g.wait_recv()
    rs[...] = (own_g + pr_g[...].astype(F32)).astype(BF)
    rg_send = give_back(rs, ret_g, rg_ss, rg_rs)

    for c in ro_send:
        c.wait_recv()
    ro = ret_o[...]
    mix[...] = (
        mm(comb[0], ro) + mm(comb[1], ro) + mm(comb[2], ro)
    ).astype(BF)

    if fused:
        at = d * blk
        total = mm_tn(
            hd[d], gr[at // half, :, pl.ds(pl.multiple_of(lax.rem(at, half), blk), blk)]
        ).astype(BF).astype(F32)
        for k in range(1, n_dp):
            hd_send[k - 1].wait_recv()
            gd_send[k - 1].wait_recv()
            src = lax.rem(d - k + n_dp, n_dp)
            total = total + mm_tn(hd[src], gd[src]).astype(BF).astype(F32)
        dgr[...] = total.astype(BF)
    else:
        for i in range(2):
            dgr[:, i * half : (i + 1) * half] = mm_tn(hidden, gr[i]).astype(BF)

    for c in rg_send:
        c.wait_recv()
    tgr[...] = mm(coll[...], ret_g[...]).astype(BF)

    for c in x_send + g_send + x_fwd + g_fwd + hd_send + gd_send + [ex_o, ex_g] + ro_send + rg_send:
        c.wait_send()


def write_kernel(a, b, c, a_out, b_out, c_out, sem):
    copies = [
        pltpu.make_async_copy(i, o, sem.at[k])
        for k, (i, o) in enumerate(((a, a_out), (b, b_out), (c, c_out)))
    ]
    for cp in copies:
        cp.start()
    for cp in copies:
        cp.wait()


def per_device(n_dp, n_ex, tokens, expert_ids, route_weight, gate_weight, up_weight, down_weight, cotangent):
    n_tok, choose = expert_ids.shape
    capacity = 3 * n_tok * choose // (2 * EXPERTS)
    cap = -(-capacity // 16) * 16
    half = tokens.shape[1]
    full = gate_weight.shape[1]
    width = gate_weight.shape[2]
    rows = n_ex * cap
    spare = cap - capacity
    parts = capacity // spare if spare and capacity % spare == 0 else 0
    if parts and half % ((parts + 1) * 128):
        parts = 0
    piece = half // (parts + 1)
    wide = parts * piece if parts else half
    blk = full // n_dp
    fused = blk % 128 == 0
    d_cols = blk if fused else full
    slots = n_dp if fused else n_dp
    gd_cols = blk if fused else 128
    vm = pltpu.VMEM
    dma = pltpu.SemaphoreType.DMA
    ne, nd = n_ex - 1, max(n_dp - 1, 1)
    hbm = pl.BlockSpec(memory_space=pl.ANY)
    inv = pl.BlockSpec(memory_space=pltpu.VMEM)
    mixed, token_grad, down = pl.pallas_call(
        functools.partial(kernel, (n_dp, n_ex, cap, capacity, parts, piece, fused)),
        out_shape=(vm((n_tok, half), BF), vm((n_tok, half), BF), vm((width, d_cols), BF)),
        in_specs=[inv, inv, hbm, hbm, hbm, hbm, hbm],
        out_specs=(inv, inv, inv),
        scratch_shapes=[
            vm((n_tok, half), BF), vm((n_tok, half), BF),
            vm((full, width), BF), vm((full, width), BF), vm((width, full), BF),
            vm((n_tok, rows), BF), vm((3, n_tok, rows), BF),
            vm((rows, wide), BF), vm((rows, wide), BF),
            vm((2, rows, wide), BF), vm((2, rows, wide), BF),
            vm((2, rows, half), BF), vm((2, rows, half), BF),
            vm((slots, rows, width), BF), vm((slots, rows, gd_cols), BF),
            vm((rows, half), BF), vm((rows, half), BF), vm((rows, half), BF), vm((rows, half), BF),
            vm((rows, half), BF), vm((rows, half), BF), vm((rows, half), BF), vm((rows, half), BF),
            dma((5,)),
            dma((ne,)), dma((ne,)), dma((ne,)), dma((ne,)),
            dma((n_ex,)), dma((n_ex,)), dma((n_ex,)), dma((n_ex,)),
            dma((nd,)), dma((nd,)), dma((nd,)), dma((nd,)),
            dma((2,)), dma((2,)),
            dma((ne,)), dma((ne,)), dma((ne,)), dma((ne,)),
        ],
        compiler_params=pltpu.CompilerParams(
            collective_id=0, has_side_effects=True, vmem_limit_bytes=56 * 1024 * 1024
        ),
    )(expert_ids.T, route_weight.T, tokens, cotangent, gate_weight, up_weight, down_weight)
    mixed, token_grad, down = pl.pallas_call(
        write_kernel,
        out_shape=tuple(jax.ShapeDtypeStruct(a.shape, BF) for a in (mixed, token_grad, down)),
        in_specs=[inv, inv, inv],
        out_specs=(hbm, hbm, hbm),
        scratch_shapes=[dma((3,))],
    )(*(pltpu.with_memory_space_constraint(a, pltpu.VMEM) for a in (mixed, token_grad, down)))
    if not fused:
        down = lax.psum_scatter(down, "dp", scatter_dimension=1, tiled=True)
    return mixed, token_grad, down[None]


def solution(mesh):
    placed = (
        P(("dp", "expert"), "tensor"),
        P(("dp", "expert"), None),
        P(("dp", "expert"), None),
        P("expert", None, "tensor"),
        P("expert", None, "tensor"),
        P("expert", "tensor", None),
        P(("dp", "expert"), "tensor"),
    )
    return jax.shard_map(
        functools.partial(per_device, mesh.shape["dp"], mesh.shape["expert"]),
        mesh=mesh,
        in_specs=placed,
        out_specs=(
            P(("dp", "expert"), "tensor"),
            P(("dp", "expert"), "tensor"),
            P("expert", "tensor", "dp"),
        ),
        check_vma=False,
    )
```

```python
import functools

import jax
import jax.numpy as jnp
from jax import lax
from jax.experimental import pallas as pl
from jax.experimental.pallas import tpu as pltpu
from jax.sharding import PartitionSpec as P

EXPERTS = 128
MESH = pl.DeviceIdType.MESH
BF = jnp.bfloat16
F32 = jnp.float32


def mm(a, b):
    return lax.dot_general(a, b, (((1,), (0,)), ((), ())), preferred_element_type=F32)


def mm_nt(a, b):
    return lax.dot_general(a, b, (((1,), (1,)), ((), ())), preferred_element_type=F32)


def mm_tn(a, b):
    return lax.dot_general(a, b, (((0,), (0,)), ((), ())), preferred_element_type=F32)


def kernel(
    dims,
    ids_ref, rw_ref, tok_hbm, cot_hbm, wg_hbm, wu_hbm, wd_hbm,
    mix, tgr, dgr,
    tok, cot, wg, wu, wd, coll, comb, xs, gs, xp, gp, xr, gr, hd, gd,
    ps_o, ps_g, pr_o, pr_g, os, rs, ret_o, ret_g,
    load_sem,
    x_ss, x_rs, g_ss, g_rs, xf_ss, xf_rs, gf_ss, gf_rs,
    hd_ss, hd_rs, gd_ss, gd_rs, ex_ss, ex_rs, ro_ss, ro_rs, rg_ss, rg_rs,
):
    n_dp, n_ex, cap, capacity, parts, piece, fused = dims
    d = lax.axis_index("dp")
    s = lax.axis_index("expert")
    t = lax.axis_index("tensor")
    other = 1 - t
    choose, n_tok = ids_ref.shape
    half = tok.shape[1]
    rows = n_ex * cap
    blk = gd.shape[2]

    def ex_peer(k):
        return {"dp": d, "expert": lax.rem(s + k, n_ex), "tensor": t}

    def dp_peer(k):
        return {"dp": lax.rem(d + k, n_dp), "expert": s, "tensor": t}

    partner = {"dp": d, "expert": s, "tensor": other}

    def block(i):
        return pl.ds(pl.multiple_of(i * cap, cap), cap)

    def half_ds(i):
        return pl.ds(pl.multiple_of(i * half, half), half)

    def remote(src, dst, ss, rs_, dev):
        return pltpu.make_async_remote_copy(
            src_ref=src, dst_ref=dst, send_sem=ss, recv_sem=rs_, device_id=dev, device_id_type=MESH
        )

    loads = [
        pltpu.make_async_copy(a, b, load_sem.at[i])
        for i, (a, b) in enumerate(
            ((tok_hbm, tok), (cot_hbm, cot), (wg_hbm.at[0], wg), (wu_hbm.at[0], wu), (wd_hbm.at[0], wd))
        )
    ]
    for c in loads:
        c.start()

    barrier = pltpu.get_barrier_semaphore()
    peers = [ex_peer(k) for k in range(1, n_ex)] + [partner]
    if fused:
        peers += [dp_peer(k) for k in range(1, n_dp)]
    for p in peers:
        pl.semaphore_signal(barrier, inc=1, device_id=p, device_id_type=MESH)

    row = lax.broadcasted_iota(jnp.int32, (rows, n_tok), 0)
    e_row = jnp.zeros((rows, n_tok), jnp.int32)
    for n in range(1, n_ex):
        e_row = e_row + jnp.where(row >= n * cap, 1, 0)
    c_row = (row - e_row * cap).astype(F32)
    chosen = jnp.zeros((rows, n_tok), F32)
    wsum = jnp.zeros((rows, n_tok), F32)
    for k in range(choose):
        hit = ids_ref[k : k + 1, :] == e_row
        chosen = chosen + jnp.where(hit, 1.0, 0.0)
        wsum = wsum + jnp.where(hit, rw_ref[k : k + 1, :], 0.0)
    earlier = lax.broadcasted_iota(jnp.int32, (n_tok, n_tok), 0) < lax.broadcasted_iota(
        jnp.int32, (n_tok, n_tok), 1
    )
    rank = mm(chosen.astype(BF), jnp.where(earlier, 1.0, 0.0).astype(BF))
    sel = jnp.where(rank == c_row, chosen, 0.0)
    wsel = sel * wsum
    sel_t = sel.astype(BF)
    w_slot = jnp.sum(wsel, axis=1, keepdims=True)

    sel_x, w_x, back = [], [], []
    if parts:
        r_sq = lax.broadcasted_iota(jnp.int32, (rows, rows), 0)
        m_sq = lax.broadcasted_iota(jnp.int32, (rows, rows), 1)
        base = jnp.zeros((rows, rows), jnp.int32)
        for n in range(1, n_ex):
            base = base + jnp.where(m_sq >= n * cap, cap, 0)
        m_c = m_sq - base
        back.append(jnp.where((r_sq == m_sq) & (m_c < capacity), 1.0, 0.0).astype(BF))
        c_int = row - e_row * cap
        for i in range(parts):
            c_i = jnp.where(c_int >= capacity, (c_int - capacity) * parts + i, -1).astype(F32)
            s_i = jnp.where(rank == c_i, chosen, 0.0)
            sel_x.append(s_i.astype(BF))
            w_x.append(jnp.sum(s_i * wsum, axis=1, keepdims=True))
            place = base + (m_c - capacity) * parts + i
            back.append(jnp.where((m_c >= capacity) & (r_sq == place), 1.0, 0.0).astype(BF))

    def pack(src, dst, weighted):
        if not parts:
            v = mm(sel_t, src[...])
            dst[...] = (v * w_slot if weighted else v).astype(BF)
        for i in range(parts):
            here = slice(i * piece, (i + 1) * piece)
            a = mm(sel_t, src[:, here])
            b = mm(sel_x[i], src[:, parts * piece :])
            dst[:, here] = (a * w_slot + b * w_x[i] if weighted else a + b).astype(BF)

    def unpack(src, dst, h):
        v = src[h]
        if not parts:
            dst[h] = v
        else:
            dst[h, :, : parts * piece] = mm(back[0], v).astype(BF)
            tail = mm(back[1], v[:, :piece])
            for i in range(1, parts):
                tail = tail + mm(back[i + 1], v[:, i * piece : (i + 1) * piece])
            dst[h, :, parts * piece :] = tail.astype(BF)

    loads[0].wait()
    pack(tok, xs, False)
    xp[t, block(s), :] = xs[block(s), :]

    pl.semaphore_wait(barrier, len(peers))

    def dispatch(src, dst, ss, rs_):
        out = []
        for k in range(1, n_ex):
            c = remote(
                src.at[block(lax.rem(s + k, n_ex))], dst.at[t, block(s)], ss.at[k - 1], rs_.at[k - 1], ex_peer(k)
            )
            c.start()
            out.append(c)
        return out

    def forwarder(dst, ss, rs_):
        out = []
        for k in range(n_ex):
            b = dst.at[t, block(lax.rem(s - k + n_ex, n_ex))]
            out.append(remote(b, b, ss.at[k], rs_.at[k], partner))
        return out

    x_send = dispatch(xs, xp, x_ss, x_rs)
    x_fwd = forwarder(xp, xf_ss, xf_rs)
    x_fwd[0].start()

    loads[1].wait()
    pack(cot, gs, True)
    gp[t, block(s), :] = gs[block(s), :]
    g_send = dispatch(gs, gp, g_ss, g_rs)
    g_fwd = forwarder(gp, gf_ss, gf_rs)
    g_fwd[0].start()

    coll[...] = sel.T.astype(BF)
    wcol = wsel.T
    w0 = wcol.astype(BF)
    r1 = wcol - w0.astype(F32)
    w1 = r1.astype(BF)
    comb[0] = w0
    comb[1] = w1
    comb[2] = (r1 - w1.astype(F32)).astype(BF)

    for k in range(1, n_ex):
        x_send[k - 1].wait_recv()
        x_fwd[k].start()
    unpack(xp, xr, t)
    loads[2].wait()
    loads[3].wait()
    gate = mm(xr[t], wg[half_ds(t), :])
    up = mm(xr[t], wu[half_ds(t), :])
    for c in x_fwd:
        c.wait_recv()
    unpack(xp, xr, other)
    gate = gate + mm(xr[other], wg[half_ds(other), :])
    up = up + mm(xr[other], wu[half_ds(other), :])
    sig = jax.nn.sigmoid(gate)
    act = gate * sig
    hidden = (act * up).astype(BF)
    hd[d] = hidden
    hd_send = []
    gd_send = []

    loads[4].wait()
    ps_o[...] = mm(hidden, wd[:, half_ds(other)]).astype(BF)
    ex_o = remote(ps_o, pr_o, ex_ss.at[0], ex_rs.at[0], partner)
    ex_o.start()
    if fused:
        for k in range(1, n_dp):
            c = remote(hd.at[d], hd.at[d], hd_ss.at[k - 1], hd_rs.at[k - 1], dp_peer(k))
            c.start()
            hd_send.append(c)
    for k in range(1, n_ex):
        g_send[k - 1].wait_recv()
        g_fwd[k].start()
    own_o = mm(hidden, wd[:, half_ds(t)]).astype(BF).astype(F32)

    def give_back(src, dst, ss, rs_):
        out = []
        for k in range(1, n_ex):
            c = remote(
                src.at[block(lax.rem(s + k, n_ex))], dst.at[block(s)], ss.at[k - 1], rs_.at[k - 1], ex_peer(k)
            )
            c.start()
            out.append(c)
        dst[block(s), :] = src[block(s), :]
        return out

    unpack(gp, gr, t)
    ex_o.wait_recv()
    os[...] = (own_o + pr_o[...].astype(F32)).astype(BF)
    ro_send = give_back(os, ret_o, ro_ss, ro_rs)

    hgrad = mm_nt(gr[t], wd[:, half_ds(t)])
    for c in g_fwd:
        c.wait_recv()
    unpack(gp, gr, other)
    hgrad = hgrad + mm_nt(gr[other], wd[:, half_ds(other)])
    gate_term = (hgrad * up * sig * (1.0 + gate * (1.0 - sig))).astype(BF)
    up_term = (hgrad * act).astype(BF)

    ps_g[...] = (
        mm_nt(gate_term, wg[half_ds(other), :]) + mm_nt(up_term, wu[half_ds(other), :])
    ).astype(BF)
    ex_g = remote(ps_g, pr_g, ex_ss.at[1], ex_rs.at[1], partner)
    ex_g.start()
    if fused:
        for k in range(1, n_dp):
            at = lax.rem(d + k, n_dp) * blk
            c = remote(
                gr.at[at // half, :, pl.ds(pl.multiple_of(lax.rem(at, half), blk), blk)],
                gd.at[d],
                gd_ss.at[k - 1],
                gd_rs.at[k - 1],
                dp_peer(k),
            )
            c.start()
            gd_send.append(c)
    own_g = (
        (mm_nt(gate_term, wg[half_ds(t), :]) + mm_nt(up_term, wu[half_ds(t), :])).astype(BF).astype(F32)
    )
    ex_g.wait_recv()
    rs[...] = (own_g + pr_g[...].astype(F32)).astype(BF)
    rg_send = give_back(rs, ret_g, rg_ss, rg_rs)

    for c in ro_send:
        c.wait_recv()
    ro = ret_o[...]
    mix[...] = (
        mm(comb[0], ro) + mm(comb[1], ro) + mm(comb[2], ro)
    ).astype(BF)

    if fused:
        at = d * blk
        total = mm_tn(
            hd[d], gr[at // half, :, pl.ds(pl.multiple_of(lax.rem(at, half), blk), blk)]
        ).astype(BF).astype(F32)
        for k in range(1, n_dp):
            hd_send[k - 1].wait_recv()
            gd_send[k - 1].wait_recv()
            src = lax.rem(d - k + n_dp, n_dp)
            total = total + mm_tn(hd[src], gd[src]).astype(BF).astype(F32)
        dgr[...] = total.astype(BF)
    else:
        for i in range(2):
            dgr[:, i * half : (i + 1) * half] = mm_tn(hidden, gr[i]).astype(BF)

    for c in rg_send:
        c.wait_recv()
    tgr[...] = mm(coll[...], ret_g[...]).astype(BF)

    for c in x_send + g_send + x_fwd + g_fwd + hd_send + gd_send + [ex_o, ex_g] + ro_send + rg_send:
        c.wait_send()


def write_kernel(a, b, c, a_out, b_out, c_out, sem):
    copies = [
        pltpu.make_async_copy(i, o, sem.at[k])
        for k, (i, o) in enumerate(((a, a_out), (b, b_out), (c, c_out)))
    ]
    for cp in copies:
        cp.start()
    for cp in copies:
        cp.wait()


def per_device(n_dp, n_ex, tokens, expert_ids, route_weight, gate_weight, up_weight, down_weight, cotangent):
    n_tok, choose = expert_ids.shape
    capacity = 3 * n_tok * choose // (2 * EXPERTS)
    cap = -(-capacity // 16) * 16
    half = tokens.shape[1]
    full = gate_weight.shape[1]
    width = gate_weight.shape[2]
    rows = n_ex * cap
    spare = cap - capacity
    parts = capacity // spare if spare and capacity % spare == 0 else 0
    if parts and half % ((parts + 1) * 128):
        parts = 0
    piece = half // (parts + 1)
    wide = parts * piece if parts else half
    blk = full // n_dp
    fused = blk % 128 == 0
    d_cols = blk if fused else full
    slots = n_dp if fused else n_dp
    gd_cols = blk if fused else 128
    vm = pltpu.VMEM
    dma = pltpu.SemaphoreType.DMA
    ne, nd = n_ex - 1, max(n_dp - 1, 1)
    hbm = pl.BlockSpec(memory_space=pl.ANY)
    inv = pl.BlockSpec(memory_space=pltpu.VMEM)
    mixed, token_grad, down = pl.pallas_call(
        functools.partial(kernel, (n_dp, n_ex, cap, capacity, parts, piece, fused)),
        out_shape=(vm((n_tok, half), BF), vm((n_tok, half), BF), vm((width, d_cols), BF)),
        in_specs=[inv, inv, hbm, hbm, hbm, hbm, hbm],
        out_specs=(inv, inv, inv),
        scratch_shapes=[
            vm((n_tok, half), BF), vm((n_tok, half), BF),
            vm((full, width), BF), vm((full, width), BF), vm((width, full), BF),
            vm((n_tok, rows), BF), vm((3, n_tok, rows), BF),
            vm((rows, wide), BF), vm((rows, wide), BF),
            vm((2, rows, wide), BF), vm((2, rows, wide), BF),
            vm((2, rows, half), BF), vm((2, rows, half), BF),
            vm((slots, rows, width), BF), vm((slots, rows, gd_cols), BF),
            vm((rows, half), BF), vm((rows, half), BF), vm((rows, half), BF), vm((rows, half), BF),
            vm((rows, half), BF), vm((rows, half), BF), vm((rows, half), BF), vm((rows, half), BF),
            dma((5,)),
            dma((ne,)), dma((ne,)), dma((ne,)), dma((ne,)),
            dma((n_ex,)), dma((n_ex,)), dma((n_ex,)), dma((n_ex,)),
            dma((nd,)), dma((nd,)), dma((nd,)), dma((nd,)),
            dma((2,)), dma((2,)),
            dma((ne,)), dma((ne,)), dma((ne,)), dma((ne,)),
        ],
        compiler_params=pltpu.CompilerParams(
            collective_id=0, has_side_effects=True, vmem_limit_bytes=56 * 1024 * 1024
        ),
    )(expert_ids.T, route_weight.T, tokens, cotangent, gate_weight, up_weight, down_weight)
    mixed, token_grad, down = pl.pallas_call(
        write_kernel,
        out_shape=tuple(jax.ShapeDtypeStruct(a.shape, BF) for a in (mixed, token_grad, down)),
        in_specs=[inv, inv, inv],
        out_specs=(hbm, hbm, hbm),
        scratch_shapes=[dma((3,))],
    )(*(pltpu.with_memory_space_constraint(a, pltpu.VMEM) for a in (mixed, token_grad, down)))
    if not fused:
        down = lax.psum_scatter(down, "dp", scatter_dimension=1, tiled=True)
    return mixed, token_grad, down[None]


def solution(mesh):
    placed = (
        P(("dp", "expert"), "tensor"),
        P(("dp", "expert"), None),
        P(("dp", "expert"), None),
        P("expert", None, "tensor"),
        P("expert", None, "tensor"),
        P("expert", "tensor", None),
        P(("dp", "expert"), "tensor"),
    )
    return jax.shard_map(
        functools.partial(per_device, mesh.shape["dp"], mesh.shape["expert"]),
        mesh=mesh,
        in_specs=placed,
        out_specs=(
            P(("dp", "expert"), "tensor"),
            P(("dp", "expert"), "tensor"),
            P("expert", "tensor", "dp"),
        ),
        check_vma=False,
    )
```
